32 devices in a mesh: tm: 8 (over z, x), head: 4 (over y, core).
Axes of the slice: x: 2, y: 2, z: 4, core: 2. Of those that a mesh axis runs over, the one named last changes fastest.
Arguments:
- query_rows: float32 [4096, 2240], P('tm', 'head'), may hold values from -6 to 6
- key_rows: float32 [4096, 2240], P('tm', 'head'), may hold values from -6 to 6
- value_rows: float32 [4096, 2240], P('tm', 'head'), may hold values from -6 to 6
- out_weight: float32 [2240, 2240], P(None, 'head'), may hold values from -0.125 to 0.125
- cotangent: float32 [4096, 2240], P('tm', 'head'), may hold values from -6 to 6
Outputs:
- grad_query: float32 [4096, 2240], P('tm', 'head')
- grad_key: float32 [4096, 2240], P('tm', 'head')
- grad_value: float32 [4096, 2240], P('tm', 'head')
- grad_weight: float32 [2240, 2240], P('tm', 'head')
The draws below stay inside these ranges and needn't reach their ends.
All inputs are finite; a program needn't handle non-finite values.
Results may differ from the reference program's by a relative error of at most 0.0003.
Values sent between devices are 32-bit elements; how exact they have to be, the bound alone decides.
A program may use at most 128 MiB of HBM per device.

```python
import jax
import jax.numpy as jnp
from jax import lax

D = 2240
HEADS = 20
HEAD_DIM = 112
TOK_DEV = 512
TOKENS = 4096
HD = 2240


def steps_of(key, extent, cuts, smallest, top_value):
    loudness, own = 1.0, jax.random.fold_in(key, 6)
    for dim, shards_of in cuts:
        draws = jnp.exp(jax.random.uniform(jax.random.fold_in(own, dim), (shards_of,), jnp.float32, smallest / len(cuts), top_value / len(cuts)))
        loudness = loudness * jnp.repeat(draws, extent[dim] // shards_of).reshape([-1 if axis == dim else 1 for axis in range(len(extent))])
    return loudness


def normal_values(stream_key, shape, scale, limit, cuts=(), dtype=jnp.bfloat16):
    entries = jax.random.normal(stream_key, shape, jnp.float32) * scale
    if len(cuts) > 0:
        entries = steps_of(stream_key, shape, cuts, -0.22, 0.18) * entries
    return jnp.clip(entries, min=-limit, max=limit).astype(dtype)


def setup_inputs(seed: int = 0) -> dict:
    key_of = jax.random.split(jax.random.key(seed), 6)
    return {
        "query_rows": normal_values(key_of[0], (TOKENS, HD), 1.0, 6.0, ((0, 8), (1, 4)), jnp.float32),
        "key_rows": normal_values(key_of[1], (TOKENS, HD), 1.0, 6.0, ((0, 8), (1, 4)), jnp.float32),
        "value_rows": normal_values(key_of[2], (TOKENS, HD), 1.0, 6.0, ((0, 8), (1, 4)), jnp.float32),
        "out_weight": normal_values(key_of[3], (D, HD), HD ** -0.5, 0.125, ((1, 4),), jnp.float32),
        "cotangent": normal_values(key_of[4], (TOKENS, D), 1.0, 6.0, ((0, 8), (1, 4)), jnp.float32),
    }


def reference(query_rows, key_rows, value_rows, out_weight, cotangent):
    highest = lax.Precision.HIGHEST
    tokens = query_rows.shape[0]
    blocks = tokens // TOK_DEV
    grad_att = jnp.dot(cotangent, out_weight, precision=highest, preferred_element_type=jnp.float32)

    def split(whole):
        return whole.reshape(blocks, TOK_DEV, HEADS, HEAD_DIM)

    causal_mask = jnp.tril(jnp.ones((TOK_DEV, TOK_DEV), jnp.float32))

    def forward(carry, items):
        state, normal = carry
        query_blk, key_blk, value_blk = items
        feat_q = jax.nn.relu(query_blk)
        feat_k = jax.nn.relu(key_blk)
        scores = jnp.einsum("thi,shi->hts", feat_q, feat_k, precision=highest) * causal_mask
        numer = jnp.einsum("hts,shj->thj", scores, value_blk, precision=highest)
        numer = numer + jnp.einsum("thi,hij->thj", feat_q, state, precision=highest)
        denom = 1.0 + jnp.sum(scores, axis=-1).T + jnp.einsum("thi,hi->th", feat_q, normal, precision=highest)
        attended = numer / denom[:, :, None]
        new_state = state + jnp.einsum("thi,thj->hij", feat_k, value_blk, precision=highest)
        new_normal = normal + jnp.sum(feat_k, axis=0)
        return (new_state, new_normal), (attended, denom, state, normal)

    zero_state = jnp.zeros((HEADS, HEAD_DIM, HEAD_DIM), jnp.float32)
    zero_normal = jnp.zeros((HEADS, HEAD_DIM), jnp.float32)
    query_b, key_b, value_b = split(query_rows), split(key_rows), split(value_rows)
    carry_end, saved = lax.scan(forward, (zero_state, zero_normal), (query_b, key_b, value_b))
    attended_b, denom_b, state_b, normal_b = saved

    def backward(carry, items):
        back, back_norm = carry
        query_blk, key_blk, value_blk, grad_blk, attended, denom, state, normal = items
        feat_q = jax.nn.relu(query_blk)
        feat_k = jax.nn.relu(key_blk)
        scores = jnp.einsum("thi,shi->hts", feat_q, feat_k, precision=highest) * causal_mask
        grad_num = grad_blk / denom[:, :, None]
        grad_den = -jnp.sum(grad_blk * attended, axis=-1) / denom
        grad_scores = (jnp.einsum("thj,shj->hts", grad_num, value_blk, precision=highest) + grad_den.T[:, :, None]) * causal_mask
        grad_fq = jnp.einsum("hts,shi->thi", grad_scores, feat_k, precision=highest)
        grad_fq = grad_fq + jnp.einsum("thj,hij->thi", grad_num, state, precision=highest) + grad_den[:, :, None] * normal[None]
        grad_fk = jnp.einsum("hts,thi->shi", grad_scores, feat_q, precision=highest)
        grad_fk = grad_fk + jnp.einsum("hij,shj->shi", back, value_blk, precision=highest) + back_norm[None]
        grad_val = jnp.einsum("hts,thj->shj", scores, grad_num, precision=highest)
        grad_val = grad_val + jnp.einsum("shi,hij->shj", feat_k, back, precision=highest)
        new_back = back + jnp.einsum("thi,thj->hij", feat_q, grad_num, precision=highest)
        new_norm = back_norm + jnp.einsum("th,thi->hi", grad_den, feat_q, precision=highest)
        grad_q = jnp.where(query_blk > 0, grad_fq, 0.0)
        grad_k = jnp.where(key_blk > 0, grad_fk, 0.0)
        return (new_back, new_norm), (grad_q, grad_k, grad_val)

    items = (query_b, key_b, value_b, split(grad_att), attended_b, denom_b, state_b, normal_b)
    carry_back, grads = lax.scan(backward, (zero_state, zero_normal), items, reverse=True)
    grad_q, grad_k, grad_val = grads
    attended_flat = attended_b.reshape(tokens, HEADS * HEAD_DIM)
    grad_weight = lax.dot_general(cotangent, attended_flat, (((0,), (0,)), ((), ())), precision=highest, preferred_element_type=jnp.float32)
    shape_out = (tokens, HEADS * HEAD_DIM)
    return grad_q.reshape(shape_out), grad_k.reshape(shape_out), grad_val.reshape(shape_out), grad_weight
```

```python
import jax
import jax.numpy as jnp
from jax import lax
from jax.sharding import PartitionSpec as P

HEAD_DIM = 112
HIGH = lax.Precision.HIGH


def ein(spec, a, b):
    return jnp.einsum(spec, a, b, precision=HIGH, preferred_element_type=jnp.float32)


def prefix(part, axis, reverse):
    count = lax.axis_size(axis)
    place = lax.axis_index(axis)
    gathered = lax.all_gather(part, axis)
    index = lax.iota(jnp.int32, count)
    wanted = index > place if reverse else index < place
    return jnp.sum(jnp.where(wanted.reshape((count,) + (1,) * part.ndim), gathered, 0.0), axis=0)


def shards(query_rows, key_rows, value_rows, out_weight, cotangent):
    rows = query_rows.shape[0]
    width = query_rows.shape[1]
    heads = width // HEAD_DIM
    shape_heads = (rows, heads, HEAD_DIM)
    whole_grad = lax.all_gather(cotangent, "head", axis=1, tiled=True)
    query = query_rows.reshape(shape_heads).transpose(1, 0, 2)
    key = key_rows.reshape(shape_heads).transpose(1, 0, 2)
    value = value_rows.reshape(shape_heads).transpose(1, 0, 2)
    feat_q = jax.nn.relu(query)
    feat_k = jax.nn.relu(key)
    ones = jnp.ones((heads, rows, 1), jnp.float32)
    value_one = jnp.concatenate([value, ones], axis=2)
    mask = jnp.tril(jnp.ones((rows, rows), jnp.bool_))
    state = prefix(ein("hti,htj->hij", feat_k, value_one), "tm", False)
    scores = jnp.where(mask, ein("hti,hsi->hts", feat_q, feat_k), 0.0)
    both = ein("hts,hsj->htj", scores, value_one) + ein("hti,hij->htj", feat_q, state)
    denom = 1.0 + both[:, :, HEAD_DIM:]
    attended = both[:, :, :HEAD_DIM] / denom
    flat = attended.transpose(1, 0, 2).reshape(rows, width)
    term = lax.dot_general(
        whole_grad,
        flat,
        (((0,), (0,)), ((), ())),
        precision=HIGH,
        preferred_element_type=jnp.float32,
    )
    grad_weight = lax.psum_scatter(term, "tm", scatter_dimension=0, tiled=True)
    grad_att = jnp.dot(
        whole_grad, out_weight, precision=HIGH, preferred_element_type=jnp.float32
    )
    grad_att = grad_att.reshape(shape_heads).transpose(1, 0, 2)
    grad_num = grad_att / denom
    grad_den = -jnp.sum(grad_att * attended, axis=2, keepdims=True) / denom
    grad_one = jnp.concatenate([grad_num, grad_den], axis=2)
    back = prefix(ein("hti,htj->hij", feat_q, grad_one), "tm", True)
    grad_scores = jnp.where(mask, ein("htj,hsj->hts", grad_one, value_one), 0.0)
    grad_fq = ein("hts,hsi->hti", grad_scores, feat_k) + ein("htj,hij->hti", grad_one, state)
    grad_fk = ein("hts,hti->hsi", grad_scores, feat_q) + ein("hsj,hij->hsi", value_one, back)
    grad_val = ein("hts,htj->hsj", scores, grad_num) + ein(
        "hsi,hij->hsj", feat_k, back[:, :, :HEAD_DIM]
    )

    def merged(a):
        return a.transpose(1, 0, 2).reshape(rows, width)

    grad_query = merged(jnp.where(query > 0, grad_fq, 0.0))
    grad_key = merged(jnp.where(key > 0, grad_fk, 0.0))
    return (grad_query, grad_key, merged(grad_val), grad_weight)


def solution(mesh):
    return jax.shard_map(
        shards,
        mesh=mesh,
        in_specs=(
            P("tm", "head"),
            P("tm", "head"),
            P("tm", "head"),
            P(None, "head"),
            P("tm", "head"),
        ),
        out_specs=(P("tm", "head"), P("tm", "head"), P("tm", "head"), P("tm", "head")),
        check_vma=False,
    )
```

```python
import jax
import jax.numpy as jnp
from jax import lax
from jax.sharding import PartitionSpec as P

HEAD_DIM = 112
HIGH = lax.Precision.HIGH


def ein(spec, a, b):
    return jnp.einsum(spec, a, b, precision=HIGH, preferred_element_type=jnp.float32)


def exchange(a, axis, bit):
    return lax.ppermute(a, axis, [(i, i ^ bit) for i in range(lax.axis_size(axis))])


def scan_others(part, axis, reverse):
    count = lax.axis_size(axis)
    place = lax.axis_index(axis)
    total = part
    others = jnp.zeros_like(part)
    bit = 1
    while bit < count:
        arrived = exchange(total, axis, bit)
        below = (place & bit) != 0
        others = others + jnp.where(jnp.logical_not(below) if reverse else below, arrived, 0.0)
        total = total + arrived
        bit *= 2
    return others


def gather_xor(block, axis):
    blocks = {0: block}
    bit = lax.axis_size(axis) // 2
    while bit:
        blocks.update({k | bit: exchange(b, axis, bit) for k, b in list(blocks.items())})
        bit //= 2
    return [blocks[k] for k in range(len(blocks))]


def halve(cube, flips, axis):
    place = lax.axis_index(axis)
    for step in range(len(flips)):
        bit = 1 << step
        dim = len(flips) - 1 - step
        mine = jnp.where((place & bit) != 0, 1, 0) ^ flips[dim]
        away = lax.dynamic_index_in_dim(cube, 1 - mine, dim, False)
        kept = lax.dynamic_index_in_dim(cube, mine, dim, False)
        cube = kept + exchange(away, axis, bit)
    return cube


def shards(query_rows, key_rows, value_rows, out_weight, cotangent):
    rows = query_rows.shape[0]
    width = query_rows.shape[1]
    heads = width // HEAD_DIM
    shape_heads = (rows, heads, HEAD_DIM)
    tm = lax.axis_size("tm")
    groups = lax.axis_size("head")
    head = lax.axis_index("head")
    grads = gather_xor(cotangent, "head")
    query = query_rows.reshape(shape_heads).transpose(1, 0, 2)
    key = key_rows.reshape(shape_heads).transpose(1, 0, 2)
    value = value_rows.reshape(shape_heads).transpose(1, 0, 2)
    feat_q = jax.nn.relu(query)
    feat_k = jax.nn.relu(key)
    ones = jnp.ones((heads, rows, 1), jnp.float32)
    value_one = jnp.concatenate([value, ones], axis=2)
    mask = jnp.tril(jnp.ones((rows, rows), jnp.bool_))
    state = scan_others(ein("hti,htj->hij", feat_k, value_one), "tm", False)
    scores = jnp.where(mask, ein("hti,hsi->hts", feat_q, feat_k), 0.0)
    both = ein("hts,hsj->htj", scores, value_one) + ein("hti,hij->htj", feat_q, state)
    denom = 1.0 + both[:, :, HEAD_DIM:]
    attended = both[:, :, :HEAD_DIM] / denom
    flat = attended.transpose(1, 0, 2).reshape(rows, width)
    share = groups * width // tm
    terms = jnp.stack([ein("td,tc->dc", g, flat) for g in grads])
    bits = tm.bit_length() - 1
    head_bits = groups.bit_length() - 1
    flips = [(head >> (head_bits - 1 - d)) & 1 for d in range(head_bits)]
    flips += [0] * (bits - head_bits)
    cut = share // 16 * 8
    pieces = []
    for low, high in ((0, cut), (cut, share)):
        piece = terms.reshape(tm, share, width)[:, low:high]
        pieces.append(halve(piece.reshape((2,) * bits + (high - low, width)), flips, "tm"))
    grad_weight = jnp.concatenate(pieces, axis=0)
    weights = out_weight.reshape(groups, width, width)
    grad_att = sum(
        ein("td,dc->tc", g, lax.dynamic_index_in_dim(weights, head ^ k, 0, False))
        for k, g in enumerate(grads)
    )
    grad_att = grad_att.reshape(shape_heads).transpose(1, 0, 2)
    grad_num = grad_att / denom
    grad_den = -jnp.sum(grad_att * attended, axis=2, keepdims=True) / denom
    grad_one = jnp.concatenate([grad_num, grad_den], axis=2)
    back = scan_others(ein("hti,htj->hij", feat_q, grad_one), "tm", True)
    grad_scores = jnp.where(mask, ein("htj,hsj->hts", grad_one, value_one), 0.0)
    grad_fq = ein("hts,hsi->hti", grad_scores, feat_k) + ein("htj,hij->hti", grad_one, state)
    grad_fk = ein("hts,hti->hsi", grad_scores, feat_q) + ein("hsj,hij->hsi", value_one, back)
    grad_val = ein("hts,htj->hsj", scores, grad_num) + ein(
        "hsi,hij->hsj", feat_k, back[:, :, :HEAD_DIM]
    )

    def merged(a):
        return a.transpose(1, 0, 2).reshape(rows, width)

    grad_query = merged(jnp.where(query > 0, grad_fq, 0.0))
    grad_key = merged(jnp.where(key > 0, grad_fk, 0.0))
    return (grad_query, grad_key, merged(grad_val), grad_weight)


def solution(mesh):
    return jax.shard_map(
        shards,
        mesh=mesh,
        in_specs=(
            P("tm", "head"),
            P("tm", "head"),
            P("tm", "head"),
            P(None, "head"),
            P("tm", "head"),
        ),
        out_specs=(P("tm", "head"), P("tm", "head"), P("tm", "head"), P("tm", "head")),
        check_vma=False,
    )
```

```python
import jax
import jax.numpy as jnp
from jax import lax
from jax.sharding import PartitionSpec as P

HEAD_DIM = 112
HIGH = lax.Precision.HIGH


def ein(spec, a, b):
    return jnp.einsum(spec, a, b, precision=HIGH, preferred_element_type=jnp.float32)


def exchange(a, axis, bit):
    return lax.ppermute(a, axis, [(i, i ^ bit) for i in range(lax.axis_size(axis))])


def scan_others(part, axis, reverse):
    count = lax.axis_size(axis)
    place = lax.axis_index(axis)
    total = part
    others = jnp.zeros_like(part)
    bit = 1
    while bit < count:
        arrived = exchange(total, axis, bit)
        below = (place & bit) != 0
        others = others + jnp.where(jnp.logical_not(below) if reverse else below, arrived, 0.0)
        total = total + arrived
        bit *= 2
    return others


def gather_xor(block, axis):
    blocks = {0: block}
    bit = lax.axis_size(axis) // 2
    while bit:
        blocks.update({k | bit: exchange(b, axis, bit) for k, b in list(blocks.items())})
        bit //= 2
    return [blocks[k] for k in range(len(blocks))]


def pieces_of(cube, order, after, held):
    place = lax.axis_index("tm")
    count = len(order)
    open_bits = list(reversed(range(count)))
    first = None
    for bit in order:
        dim = open_bits.index(bit)
        open_bits.remove(bit)
        mine = jnp.where((place & (1 << bit)) != 0, 1, 0)
        away = lax.dynamic_index_in_dim(cube, 1 - mine, dim, False)
        kept = lax.dynamic_index_in_dim(cube, mine, dim, False)
        if first is None and after is not None:
            away, _ = lax.optimization_barrier((away, after))
        if first is None and after is None:
            away, held = lax.optimization_barrier((away, held))
        arrived = exchange(away, "tm", 1 << bit)
        first = arrived if first is None else first
        cube = kept + arrived
    return cube, first, held


def shards(query_rows, key_rows, value_rows, out_weight, cotangent):
    rows = query_rows.shape[0]
    width = query_rows.shape[1]
    heads = width // HEAD_DIM
    shape_heads = (rows, heads, HEAD_DIM)
    tm = lax.axis_size("tm")
    groups = lax.axis_size("head")
    head = lax.axis_index("head")
    whole_grad = jnp.zeros((rows, groups * width), jnp.float32)
    for k, block in enumerate(gather_xor(cotangent, "head")):
        whole_grad = lax.dynamic_update_slice_in_dim(whole_grad, block, (head ^ k) * width, 1)
    grad_att = jnp.dot(whole_grad, out_weight, precision=HIGH, preferred_element_type=jnp.float32)
    query = query_rows.reshape(shape_heads).transpose(1, 0, 2)
    key = key_rows.reshape(shape_heads).transpose(1, 0, 2)
    value = value_rows.reshape(shape_heads).transpose(1, 0, 2)
    feat_q = jax.nn.relu(query)
    feat_k = jax.nn.relu(key)
    ones = jnp.ones((heads, rows, 1), jnp.float32)
    value_one = jnp.concatenate([value, ones], axis=2)
    mask = jnp.tril(jnp.ones((rows, rows), jnp.bool_))
    state = scan_others(ein("hti,htj->hij", feat_k, value_one), "tm", False)
    scores = jnp.where(mask, ein("hti,hsi->hts", feat_q, feat_k), 0.0)
    both = ein("hts,hsj->htj", scores, value_one) + ein("hti,hij->htj", feat_q, state)
    denom = 1.0 + both[:, :, HEAD_DIM:]
    attended = both[:, :, :HEAD_DIM] / denom
    flat = attended.transpose(1, 0, 2).reshape(rows, width)
    flat, grad_att = lax.optimization_barrier((flat, grad_att))
    terms = ein("tgd,tc->gdc", whole_grad.reshape(rows, tm, -1), flat)
    share = groups * width // tm
    bits = tm.bit_length() - 1
    cut = share * 2 // 40 * 8
    up = list(range(bits))
    parts = []
    arrived = None
    for low, high, order in ((0, cut, up), (cut, 2 * cut, up), (2 * cut, share, up[1:] + up[:1])):
        piece = terms[:, low:high].reshape((2,) * bits + (high - low, width))
        part, first, grad_att = pieces_of(piece, order, arrived if low == cut else None, grad_att)
        arrived = first if low == 0 else arrived
        parts.append(part)
    grad_weight = jnp.concatenate(parts, axis=0)
    grad_att = grad_att.reshape(shape_heads).transpose(1, 0, 2)
    grad_num = grad_att / denom
    grad_den = -jnp.sum(grad_att * attended, axis=2, keepdims=True) / denom
    grad_one = jnp.concatenate([grad_num, grad_den], axis=2)
    back = scan_others(ein("hti,htj->hij", feat_q, grad_one), "tm", True)
    grad_scores = jnp.where(mask, ein("htj,hsj->hts", grad_one, value_one), 0.0)
    grad_fq = ein("hts,hsi->hti", grad_scores, feat_k) + ein("htj,hij->hti", grad_one, state)
    grad_fk = ein("hts,hti->hsi", grad_scores, feat_q) + ein("hsj,hij->hsi", value_one, back)
    grad_val = ein("hts,htj->hsj", scores, grad_num) + ein(
        "hsi,hij->hsj", feat_k, back[:, :, :HEAD_DIM]
    )

    def merged(a):
        return a.transpose(1, 0, 2).reshape(rows, width)

    grad_query = merged(jnp.where(query > 0, grad_fq, 0.0))
    grad_key = merged(jnp.where(key > 0, grad_fk, 0.0))
    return (grad_query, grad_key, merged(grad_val), grad_weight)


def solution(mesh):
    return jax.shard_map(
        shards,
        mesh=mesh,
        in_specs=(
            P("tm", "head"),
            P("tm", "head"),
            P("tm", "head"),
            P(None, "head"),
            P("tm", "head"),
        ),
        out_specs=(P("tm", "head"), P("tm", "head"), P("tm", "head"), P("tm", "head")),
        check_vma=False,
    )
```

```python
import jax
import jax.numpy as jnp
from jax import lax
from jax.sharding import PartitionSpec as P

HEAD_DIM = 112
HIGH = lax.Precision.HIGH


def ein(spec, a, b):
    return jnp.einsum(spec, a, b, precision=HIGH, preferred_element_type=jnp.float32)


def exchange(a, axis, bit):
    return lax.ppermute(a, axis, [(i, i ^ bit) for i in range(lax.axis_size(axis))])


def scan_others(part, axis, reverse):
    count = lax.axis_size(axis)
    place = lax.axis_index(axis)
    total = part
    others = jnp.zeros_like(part)
    bit = 1
    while bit < count:
        arrived = exchange(total, axis, bit)
        below = (place & bit) != 0
        others = others + jnp.where(jnp.logical_not(below) if reverse else below, arrived, 0.0)
        total = total + arrived
        bit *= 2
    return others


def gather_xor(block, axis):
    blocks = {0: block}
    bit = lax.axis_size(axis) // 2
    while bit:
        blocks.update({k | bit: exchange(b, axis, bit) for k, b in list(blocks.items())})
        bit //= 2
    return [blocks[k] for k in range(len(blocks))]


def split(cube, left, bit):
    dim = left.index(bit)
    mine = jnp.where((lax.axis_index("tm") & (1 << bit)) != 0, 1, 0)
    away = lax.dynamic_index_in_dim(cube, 1 - mine, dim, False)
    kept = lax.dynamic_index_in_dim(cube, mine, dim, False)
    return away, kept, [x for x in left if x != bit]


def finish(cube, left, order, gate):
    for bit in order:
        away, kept, left = split(cube, left, bit)
        if gate is not None:
            away, _ = lax.optimization_barrier((away, gate))
            gate = None
        cube = kept + exchange(away, "tm", 1 << bit)
    return cube


def shards(query_rows, key_rows, value_rows, out_weight, cotangent):
    rows = query_rows.shape[0]
    width = query_rows.shape[1]
    heads = width // HEAD_DIM
    shape_heads = (rows, heads, HEAD_DIM)
    tm = lax.axis_size("tm")
    groups = lax.axis_size("head")
    head = lax.axis_index("head")
    whole_grad = jnp.zeros((rows, groups * width), jnp.float32)
    for k, block in enumerate(gather_xor(cotangent, "head")):
        whole_grad = lax.dynamic_update_slice_in_dim(whole_grad, block, (head ^ k) * width, 1)
    query = query_rows.reshape(shape_heads).transpose(1, 0, 2)
    key = key_rows.reshape(shape_heads).transpose(1, 0, 2)
    value = value_rows.reshape(shape_heads).transpose(1, 0, 2)
    feat_q = jax.nn.relu(query)
    feat_k = jax.nn.relu(key)
    ones = jnp.ones((heads, rows, 1), jnp.float32)
    value_one = jnp.concatenate([value, ones], axis=2)
    mask = jnp.tril(jnp.ones((rows, rows), jnp.bool_))
    state = scan_others(ein("hti,htj->hij", feat_k, value_one), "tm", False)
    scores = jnp.where(mask, ein("hti,hsi->hts", feat_q, feat_k), 0.0)
    both = ein("hts,hsj->htj", scores, value_one) + ein("hti,hij->htj", feat_q, state)
    denom = 1.0 + both[:, :, HEAD_DIM:]
    attended = both[:, :, :HEAD_DIM] / denom
    flat = attended.transpose(1, 0, 2).reshape(rows, width)
    terms = ein("tgd,tc->gdc", whole_grad.reshape(rows, tm, -1), flat)
    share = groups * width // tm
    bits = tm.bit_length() - 1
    cut = share * 2 // 40 * 8
    up = list(range(bits))
    around = up[1:] + up[:1]
    left = up[::-1]

    def cube_of(low, high):
        return terms[:, low:high].reshape((2,) * bits + (high - low, width))

    away_a, kept_a, left_a = split(cube_of(0, cut), left, up[0])
    away_c, kept_c, left_c = split(cube_of(2 * cut, share), left, around[0])
    away_a, away_c, whole_late = lax.optimization_barrier((away_a, away_c, whole_grad))
    arrived_a = exchange(away_a, "tm", 1 << up[0])
    arrived_c = exchange(away_c, "tm", 1 << around[0])
    grad_att = jnp.dot(whole_late, out_weight, precision=HIGH, preferred_element_type=jnp.float32)
    grad_att, arrived_c = lax.optimization_barrier((grad_att, arrived_c))
    part_b = finish(cube_of(cut, 2 * cut), left, up, arrived_a)
    part_a = finish(kept_a + arrived_a, left_a, up[1:], None)
    part_c = finish(kept_c + arrived_c, left_c, around[1:], arrived_a)
    grad_weight = jnp.concatenate([part_a, part_b, part_c], axis=0)
    grad_att = grad_att.reshape(shape_heads).transpose(1, 0, 2)
    grad_num = grad_att / denom
    grad_den = -jnp.sum(grad_att * attended, axis=2, keepdims=True) / denom
    grad_one = jnp.concatenate([grad_num, grad_den], axis=2)
    back = scan_others(ein("hti,htj->hij", feat_q, grad_one), "tm", True)
    grad_scores = jnp.where(mask, ein("htj,hsj->hts", grad_one, value_one), 0.0)
    grad_scores, scores, _ = lax.optimization_barrier((grad_scores, scores, arrived_a))
    grad_fq = ein("hts,hsi->hti", grad_scores, feat_k) + ein("htj,hij->hti", grad_one, state)
    grad_fk = ein("hts,hti->hsi", grad_scores, feat_q) + ein("hsj,hij->hsi", value_one, back)
    grad_val = ein("hts,htj->hsj", scores, grad_num) + ein(
        "hsi,hij->hsj", feat_k, back[:, :, :HEAD_DIM]
    )

    def merged(a):
        return a.transpose(1, 0, 2).reshape(rows, width)

    grad_query = merged(jnp.where(query > 0, grad_fq, 0.0))
    grad_key = merged(jnp.where(key > 0, grad_fk, 0.0))
    return (grad_query, grad_key, merged(grad_val), grad_weight)


def solution(mesh):
    return jax.shard_map(
        shards,
        mesh=mesh,
        in_specs=(
            P("tm", "head"),
            P("tm", "head"),
            P("tm", "head"),
            P(None, "head"),
            P("tm", "head"),
        ),
        out_specs=(P("tm", "head"), P("tm", "head"), P("tm", "head"), P("tm", "head")),
        check_vma=False,
    )
```

```python
import jax
import jax.numpy as jnp
from jax import lax
from jax.sharding import PartitionSpec as P

HEAD_DIM = 112
HIGH = lax.Precision.HIGH


def ein(spec, a, b):
    return jnp.einsum(spec, a, b, precision=HIGH, preferred_element_type=jnp.float32)


def exchange(a, axis, bit):
    return lax.ppermute(a, axis, [(i, i ^ bit) for i in range(lax.axis_size(axis))])


def scan_others(part, axis, reverse):
    count = lax.axis_size(axis)
    place = lax.axis_index(axis)
    total = part
    others = jnp.zeros_like(part)
    bit = 1
    while bit < count:
        arrived = exchange(total, axis, bit)
        below = (place & bit) != 0
        others = others + jnp.where(jnp.logical_not(below) if reverse else below, arrived, 0.0)
        total = total + arrived
        bit *= 2
    return others


def gather_xor(block, axis):
    blocks = {0: block}
    bit = lax.axis_size(axis) // 2
    while bit:
        blocks.update({k | bit: exchange(b, axis, bit) for k, b in list(blocks.items())})
        bit //= 2
    return [blocks[k] for k in range(len(blocks))]


def split(cube, left, bit):
    dim = left.index(bit)
    mine = jnp.where((lax.axis_index("tm") & (1 << bit)) != 0, 1, 0)
    away = lax.dynamic_index_in_dim(cube, 1 - mine, dim, False)
    kept = lax.dynamic_index_in_dim(cube, mine, dim, False)
    return away, kept, [x for x in left if x != bit]


def finish(cube, left, order, gate):
    for bit in order:
        away, kept, left = split(cube, left, bit)
        if gate is not None:
            away, _ = lax.optimization_barrier((away, gate))
            gate = None
        cube = kept + exchange(away, "tm", 1 << bit)
    return cube


def shards(query_rows, key_rows, value_rows, out_weight, cotangent):
    rows = query_rows.shape[0]
    width = query_rows.shape[1]
    heads = width // HEAD_DIM
    shape_heads = (rows, heads, HEAD_DIM)
    tm = lax.axis_size("tm")
    groups = lax.axis_size("head")
    head = lax.axis_index("head")
    whole_grad = jnp.zeros((rows, groups * width), jnp.float32)
    for k, block in enumerate(gather_xor(cotangent, "head")):
        whole_grad = lax.dynamic_update_slice_in_dim(whole_grad, block, (head ^ k) * width, 1)
    query = query_rows.reshape(shape_heads).transpose(1, 0, 2)
    key = key_rows.reshape(shape_heads).transpose(1, 0, 2)
    value = value_rows.reshape(shape_heads).transpose(1, 0, 2)
    feat_q = jax.nn.relu(query)
    feat_k = jax.nn.relu(key)
    ones = jnp.ones((heads, rows, 1), jnp.float32)
    value_one = jnp.concatenate([value, ones], axis=2)
    mask = jnp.tril(jnp.ones((rows, rows), jnp.bool_))
    state = scan_others(ein("hti,htj->hij", feat_k, value_one), "tm", False)
    scores = jnp.where(mask, ein("hti,hsi->hts", feat_q, feat_k), 0.0)
    both = ein("hts,hsj->htj", scores, value_one) + ein("hti,hij->htj", feat_q, state)
    denom = 1.0 + both[:, :, HEAD_DIM:]
    attended = both[:, :, :HEAD_DIM] / denom
    flat = attended.transpose(1, 0, 2).reshape(rows, width)
    terms = ein("tgd,tc->gdc", whole_grad.reshape(rows, tm, -1), flat)
    share = groups * width // tm
    bits = tm.bit_length() - 1
    cut = share * 3 // 7 // 8 * 8
    last = share * 27 // 35 // 8 * 8
    up = list(range(bits))
    around = up[1:] + up[:1]
    left = up[::-1]

    def cube_of(low, high):
        return terms[:, low:high].reshape((2,) * bits + (high - low, width))

    away_a, kept_a, left_a = split(cube_of(0, cut), left, up[0])
    away_c, kept_c, left_c = split(cube_of(last, share), left, around[0])
    away_a, away_c, whole_late = lax.optimization_barrier((away_a, away_c, whole_grad))
    arrived_a = exchange(away_a, "tm", 1 << up[0])
    arrived_c = exchange(away_c, "tm", 1 << around[0])
    grad_att = jnp.dot(whole_late, out_weight, precision=HIGH, preferred_element_type=jnp.float32)
    grad_att, arrived_c = lax.optimization_barrier((grad_att, arrived_c))
    part_b = finish(cube_of(cut, last), left, up, arrived_a)
    part_a = finish(kept_a + arrived_a, left_a, up[1:], None)
    part_c = finish(kept_c + arrived_c, left_c, around[1:], None)
    grad_weight = jnp.concatenate([part_a, part_b, part_c], axis=0)
    grad_att = grad_att.reshape(shape_heads).transpose(1, 0, 2)
    grad_num = grad_att / denom
    grad_den = -jnp.sum(grad_att * attended, axis=2, keepdims=True) / denom
    grad_one = jnp.concatenate([grad_num, grad_den], axis=2)
    local_back = ein("hti,htj->hij", feat_q, grad_one)
    local_back, _ = lax.optimization_barrier((local_back, arrived_a))
    back = scan_others(local_back, "tm", True)
    grad_scores = jnp.where(mask, ein("htj,hsj->hts", grad_one, value_one), 0.0)
    grad_scores, scores, _ = lax.optimization_barrier((grad_scores, scores, arrived_a))
    grad_fq = ein("hts,hsi->hti", grad_scores, feat_k) + ein("htj,hij->hti", grad_one, state)
    grad_fk = ein("hts,hti->hsi", grad_scores, feat_q) + ein("hsj,hij->hsi", value_one, back)
    grad_val = ein("hts,htj->hsj", scores, grad_num) + ein(
        "hsi,hij->hsj", feat_k, back[:, :, :HEAD_DIM]
    )

    def merged(a):
        return a.transpose(1, 0, 2).reshape(rows, width)

    grad_query = merged(jnp.where(query > 0, grad_fq, 0.0))
    grad_key = merged(jnp.where(key > 0, grad_fk, 0.0))
    return (grad_query, grad_key, merged(grad_val), grad_weight)


def solution(mesh):
    return jax.shard_map(
        shards,
        mesh=mesh,
        in_specs=(
            P("tm", "head"),
            P("tm", "head"),
            P("tm", "head"),
            P(None, "head"),
            P("tm", "head"),
        ),
        out_specs=(P("tm", "head"), P("tm", "head"), P("tm", "head"), P("tm", "head")),
        check_vma=False,
    )
```
